32 devices in a mesh: blk: 4 (over x, core), grp: 8 (over z, y).
Axes of the slice: x: 2, y: 2, z: 4, core: 2. Of those that a mesh axis runs over, the one named last changes fastest.
Arguments:
- amplitudes: bfloat16 [1536, 1024], P(('blk', 'grp')), may hold values from -6 to 6
- integrals: bfloat16 [1024, 8192], P(None, ('grp', 'blk')), may hold values from -0.1875 to 0.1875
- amplitude_mask: int32 [96, 8], P(('blk', 'grp')), may hold values 0 or 1
- integral_mask: int32 [8, 64], P(None, ('grp', 'blk')), may hold values 0 or 1
Outputs:
- residual: bfloat16 [1536, 8192], P('blk', 'grp')
The draws below stay inside these ranges and needn't reach their ends.
All inputs are finite; a program needn't handle non-finite values. No bound on the sum of `amplitude_mask` or of `integral_mask` on one device may be relied on, other than what follows from the above.
Results may differ from the reference program's by a relative error of at most 0.001.
Values may be sent and summed in bfloat16 or wider, within the bound.
No kernel may reach another device: no remote copies, remote signals or barrier semaphores. Data moves between devices by JAX's collectives and lax.ppermute only.
A program may use at most 64 MiB of HBM per device.

```python
import jax
import jax.numpy as jnp
from jax import lax

TILE = 128
OTILE = 16
CD_TILES = 8
CD = 1024
OP = 1536
AB = 8192
N_BLK = 4


def set_ends(values, stream_key, low, top_value):
    shape = values.shape
    index_at = [jax.random.randint(jax.random.fold_in(stream_key, axis), (), 0, shape[axis]) for axis in range(len(shape))]
    values = values.at[tuple(index_at)].set(low)
    longest = shape.index(max(shape))
    index_at[longest] = (index_at[longest] + 1) % shape[longest]
    return values.at[tuple(index_at)].set(top_value)


def levels(stream_key, extent, split, least, largest):
    def one(axis_at, parts):
        draws = jax.random.uniform(jax.random.fold_in(jax.random.fold_in(stream_key, 6), axis_at), (parts,), jnp.float32, least / len(split), largest / len(split))
        return jnp.repeat(jnp.exp(draws), extent[axis_at] // parts).reshape((-1,) + (1,) * (len(extent) - axis_at - 1))

    gain = one(*split[0])
    for cut in split[1:]:
        gain = gain * one(*cut)
    return gain


def gaussian(key, dims, scale, reach, cuts=(), kind=jnp.bfloat16):
    factor_of = levels(key, dims, cuts, -0.22, 0.18) if cuts else 1.0
    entries = jax.random.normal(key, dims, jnp.float32) * scale * factor_of
    return jnp.minimum(jnp.maximum(entries, -reach), reach).astype(kind)


def setup_inputs(seed: int = 0) -> dict:
    key_list = jax.random.split(jax.random.key(seed), 5)
    amplitudes = gaussian(key_list[0], (OP, CD), 1.0, 6.0, ((0, 32),))
    integrals = gaussian(key_list[1], (CD, AB), CD ** -0.5, 0.1875, ((1, 32),))
    amplitude_mask = set_ends((jax.random.randint(key_list[2], (OP // OTILE, CD_TILES), 0, 4) < 3).astype(jnp.int32), jax.random.fold_in(key_list[2], 1), 0, 1)
    integral_mask = set_ends((jax.random.randint(key_list[3], (CD_TILES, AB // TILE), 0, 4) < 3).astype(jnp.int32), jax.random.fold_in(key_list[3], 1), 0, 1)
    return {"amplitudes": amplitudes, "integrals": integrals, "amplitude_mask": amplitude_mask, "integral_mask": integral_mask}


def mask_tiles(values, screen, row_tile, col_tile):
    height, breadth = values.shape
    tiled = values.reshape(height // row_tile, row_tile, breadth // col_tile, col_tile)
    tiled = tiled * screen.astype(values.dtype)[:, None, :, None]
    return tiled.reshape(height, breadth)


def reference(amplitudes, integrals, amplitude_mask, integral_mask):
    amp_masked = mask_tiles(amplitudes, amplitude_mask, OTILE, TILE)
    int_masked = mask_tiles(integrals, integral_mask, TILE, TILE)
    row_blocks = amp_masked.reshape(N_BLK, OP // N_BLK, CD)

    def block_product(block_rows):
        return (0.5 * jnp.dot(block_rows, int_masked, preferred_element_type=jnp.float32)).astype(jnp.bfloat16)

    return lax.map(block_product, row_blocks).reshape(OP, AB)
```

```python
import functools
import jax
import jax.numpy as jnp
from jax import lax
from jax.experimental import pallas as pl
from jax.experimental.pallas import tpu as pltpu
from jax.sharding import PartitionSpec as P

TILE = 128
OTILE = 16
VMEM = pl.BlockSpec(memory_space=pltpu.VMEM)
SMEM = pl.BlockSpec(memory_space=pltpu.SMEM)


def limit(*values):
    nbytes = sum(v.size * v.dtype.itemsize for v in values)
    return pltpu.CompilerParams(vmem_limit_bytes=2 * nbytes + 4 * 2**20)


def after(v, *deps):
    return lax.optimization_barrier((v, *deps))[0]


def held(v):
    return pltpu.with_memory_space_constraint(v, pltpu.VMEM)


def mask_kernel(amask, bmask, a, b, a_out, b_out):
    def factor(mask, i, j):
        return mask[i, j].astype(jnp.float32).astype(a.dtype)

    for i in range(a.shape[0] // OTILE):
        for j in range(a.shape[1] // TILE):
            at = (slice(i * OTILE, (i + 1) * OTILE), slice(j * TILE, (j + 1) * TILE))
            a_out[at] = a[at] * factor(amask, i, j)
    for i in range(b.shape[0] // TILE):
        for j in range(b.shape[1] // TILE):
            at = (slice(i * TILE, (i + 1) * TILE), slice(j * TILE, (j + 1) * TILE))
            b_out[at] = b[at] * factor(bmask, j, i)


def product_kernel(n_grp, n_blk, *refs):
    a_refs, b_refs, (out, a_all, o_all, sems) = refs[:n_grp], refs[n_grp:-4], refs[-4:]
    g, q = lax.axis_index("grp"), lax.axis_index("blk")
    rows = a_refs[0].shape[0]
    for k, ref in enumerate(a_refs):
        a_all[pl.ds(pl.multiple_of((g ^ k) * rows, OTILE), rows), :] = ref[...]
    width = b_refs[0].shape[1]
    copies = []
    for k in range(n_blk):
        acc = jnp.dot(a_all[...], b_refs[k][...], preferred_element_type=jnp.float32)
        o_all[k] = (0.5 * acc).astype(out.dtype)
        cols = pl.ds(pl.multiple_of((q ^ k) * width, TILE), width)
        copies.append(pltpu.make_async_copy(o_all.at[k], out.at[:, cols], sems.at[k]))
        copies[-1].start()
    for c in copies:
        c.wait()


def local(n_blk, n_grp, a, b, amask, bmask):
    a_own, b_own = pl.pallas_call(
        mask_kernel,
        out_shape=[pltpu.VMEM(a.shape, a.dtype), pltpu.VMEM(b.shape, b.dtype)],
        in_specs=[SMEM, SMEM, VMEM, VMEM],
        out_specs=[VMEM, VMEM],
        compiler_params=limit(a, b),
    )(amask, bmask.T, a, b)

    def swap(v, axis, n, k):
        return lax.ppermute(v, axis, [(i, i ^ k) for i in range(n)])

    far = {k: swap(b_own, "blk", n_blk, k) for k in range(2, n_blk, 2)}
    direct = [1 << i for i in reversed(range(n_grp.bit_length() - 1))]
    got = lax.optimization_barrier([swap(a_own, "grp", n_grp, k) for k in direct])
    a_all = {0: a_own, **dict(zip(direct, got, strict=True))}
    for top in reversed(direct):
        for k in (*range(top // 2, top), *range(1, top // 2)):
            if k:
                a_all[top ^ k] = swap(a_all[top], "grp", n_grp, k)
    b_all = {0: b_own, 1: swap(after(b_own, a_all[n_grp * 3 // 4]), "blk", n_blk, 1)}
    for k, v in far.items():
        b_all |= {k: v, k ^ 1: swap(after(v, *a_all.values()), "blk", n_blk, 1)}
    a_all, b_all = ([d[k] for k in sorted(d)] for d in (a_all, b_all))
    rows, cols = a.shape[0] * n_grp, b.shape[1] * n_blk
    ops = [held(v) for v in a_all + b_all]
    out = jax.ShapeDtypeStruct((rows, cols), a.dtype)
    return pl.pallas_call(
        functools.partial(product_kernel, n_grp, n_blk),
        out_shape=out,
        in_specs=[VMEM] * len(ops),
        out_specs=pl.BlockSpec(memory_space=pl.ANY),
        scratch_shapes=[
            pltpu.VMEM((rows, a.shape[1]), a.dtype),
            pltpu.VMEM((n_blk, rows, b.shape[1]), a.dtype),
            pltpu.SemaphoreType.DMA((n_blk,)),
        ],
        compiler_params=limit(out, *a_all),
    )(*ops)


def solution(mesh):
    return jax.shard_map(
        functools.partial(local, mesh.shape["blk"], mesh.shape["grp"]),
        mesh=mesh,
        in_specs=(
            P(("blk", "grp"), None),
            P(None, ("grp", "blk")),
            P(("blk", "grp"), None),
            P(None, ("grp", "blk")),
        ),
        out_specs=P("blk", "grp"),
        check_vma=False,
    )
```

```python
import functools
import jax
import jax.numpy as jnp
from jax import lax
from jax.experimental import pallas as pl
from jax.experimental.pallas import tpu as pltpu
from jax.sharding import PartitionSpec as P

TILE = 128
OTILE = 16
VMEM = pl.BlockSpec(memory_space=pltpu.VMEM)
SMEM = pl.BlockSpec(memory_space=pltpu.SMEM)
ANY = pl.BlockSpec(memory_space=pl.ANY)


def limit(*values):
    nbytes = sum(v.size * v.dtype.itemsize for v in values)
    return pltpu.CompilerParams(vmem_limit_bytes=2 * nbytes + 4 * 2**20)


def after(v, *deps):
    return lax.optimization_barrier((v, *deps))[0]


def held(v):
    return pltpu.with_memory_space_constraint(v, pltpu.VMEM)


def mask_kernel(amask, bmask, a, b, a_out, b_out):
    def factor(mask, i, j):
        return mask[i, j].astype(jnp.float32).astype(a.dtype)

    for i in range(a.shape[0] // OTILE):
        for j in range(a.shape[1] // TILE):
            at = (slice(i * OTILE, (i + 1) * OTILE), slice(j * TILE, (j + 1) * TILE))
            a_out[at] = a[at] * factor(amask, i, j)
    for i in range(b.shape[0] // TILE):
        for j in range(b.shape[1] // TILE):
            at = (slice(i * TILE, (i + 1) * TILE), slice(j * TILE, (j + 1) * TILE))
            b_out[at] = b[at] * factor(bmask, j, i)


def product(a, b, dtype):
    return (0.5 * jnp.dot(a, b, preferred_element_type=jnp.float32)).astype(dtype)


def near_kernel(masks, *refs):
    a_refs, b_refs, (a_all, near) = refs[: len(masks)], refs[len(masks) : -2], refs[-2:]
    for ks, ref in zip(masks, a_refs, strict=True):
        rows = ref.shape[0] // len(ks)
        for i, k in enumerate(ks):
            at = pl.multiple_of((lax.axis_index("grp") ^ k) * rows, OTILE)
            a_all[pl.ds(at, rows), :] = ref[i * rows : (i + 1) * rows, :]
    for n, b in enumerate(b_refs):
        near[n] = product(a_all[...], b[...], near.dtype)


def far_kernel(near_at, far_at, a_all, near, *refs):
    b_refs, (out, stage, near_sems, far_sems) = refs[:-4], refs[-4:]
    rows, width = near.shape[1:]

    def write(block, k, top, sem):
        at = pl.multiple_of((lax.axis_index("blk") ^ k) * width, TILE)
        copy = pltpu.make_async_copy(block, out.at[pl.ds(top, block.shape[0]), pl.ds(at, width)], sem)
        copy.start()
        return copy

    copies = [write(near.at[n], k, 0, near_sems.at[n]) for n, k in enumerate(near_at)]
    cuts = far_sems.shape[1]
    for n, k in enumerate(far_at):
        for c in range(cuts):
            at = pl.ds(c * (rows // cuts), rows // cuts)
            stage[n, at, :] = product(a_all[at, :], b_refs[n][...], stage.dtype)
            copies.append(write(stage.at[n, at], k, c * (rows // cuts), far_sems.at[n, c]))
    for copy in copies:
        copy.wait()


def local(n_blk, n_grp, a, b, amask, bmask):
    a_own, b_own = pl.pallas_call(
        mask_kernel,
        out_shape=[pltpu.VMEM(a.shape, a.dtype), pltpu.VMEM(b.shape, b.dtype)],
        in_specs=[SMEM, SMEM, VMEM, VMEM],
        out_specs=[VMEM, VMEM],
        compiler_params=pltpu.CompilerParams(vmem_limit_bytes=56 * 2**20),
    )(amask, bmask.T, a, b)

    def swap(v, axis, n, k):
        return lax.ppermute(v, axis, [(i, i ^ k) for i in range(n)])

    def joined(*vs):
        def join_kernel(*refs):
            top = 0
            for ref in refs[:-1]:
                refs[-1][top : top + ref.shape[0], :] = ref[...]
                top += ref.shape[0]

        rows = sum(v.shape[0] for v in vs)
        return pl.pallas_call(
            join_kernel,
            out_shape=pltpu.VMEM((rows, vs[0].shape[1]), vs[0].dtype),
            in_specs=[VMEM] * len(vs),
            out_specs=VMEM,
            compiler_params=limit(*vs),
        )(*[held(v) for v in vs])

    def line(*vs):
        done = []
        for v in vs:
            done = list(lax.optimization_barrier((v, *done)))
        return done[::-1]

    def along_grp(v, k):
        return swap(v, "grp", n_grp, k)

    def along_blk(v, k):
        return swap(v, "blk", n_blk, k)

    panels = {0: b_own} | {k: along_blk(b_own, k) for k in range(2, n_blk, 2)}
    z4, z2, z1 = along_grp(a_own, 4), along_grp(a_own, 2), along_grp(a_own, 1)
    z4, z2 = line(z4, z2)
    pair = joined(z2, z4)
    m7 = along_grp(z4, 3)
    m35 = along_grp(after(pair, z1), 1)
    m6 = along_grp(after(z4, z1), 2)
    panels |= {k ^ 1: along_blk(after(v, z1), 1) for k, v in panels.items()}
    m7, m35, m6 = line(m7, m35, m6)
    shards = {(0,): a_own, (1,): z1, (2,): z2, (3, 5): m35, (4,): z4, (6,): m6, (7,): m7}
    for top in [8 << i for i in range((n_grp // 8).bit_length() - 1)]:
        shards[(top,)] = along_grp(a_own, top)
        shards |= {(top ^ k,): along_grp(shards[(top,)], k) for k in range(1, top)}
    rows, depth, width = a.shape[0] * n_grp, a.shape[1], b.shape[1]
    out = jax.ShapeDtypeStruct((rows, width * n_blk), a.dtype)
    near_at, far_at = list(range(0, n_blk, 2)), list(range(1, n_blk, 2))
    a_full, near = pl.pallas_call(
        functools.partial(near_kernel, list(shards)),
        out_shape=[pltpu.VMEM((rows, depth), a.dtype), pltpu.VMEM((len(near_at), rows, width), a.dtype)],
        in_specs=[VMEM] * (len(shards) + len(near_at)),
        out_specs=[VMEM, VMEM],
        compiler_params=limit(out),
        cost_estimate=pl.CostEstimate(flops=50 * 10**8, bytes_accessed=2**22, transcendentals=0),
    )(*[held(v) for v in [*shards.values()] + [panels[k] for k in near_at]])
    return pl.pallas_call(
        functools.partial(far_kernel, near_at, far_at),
        out_shape=out,
        in_specs=[VMEM] * (2 + len(far_at)),
        out_specs=ANY,
        scratch_shapes=[
            pltpu.VMEM((len(far_at), rows, width), a.dtype),
            pltpu.SemaphoreType.DMA((len(near_at),)),
            pltpu.SemaphoreType.DMA((len(far_at), 2)),
        ],
        compiler_params=limit(out),
    )(*[held(v) for v in [a_full, near] + [panels[k] for k in far_at]])


def solution(mesh):
    return jax.shard_map(
        functools.partial(local, mesh.shape["blk"], mesh.shape["grp"]),
        mesh=mesh,
        in_specs=(
            P(("blk", "grp"), None),
            P(None, ("grp", "blk")),
            P(("blk", "grp"), None),
            P(None, ("grp", "blk")),
        ),
        out_specs=P("blk", "grp"),
        check_vma=False,
    )
```

```python
import functools
import jax
import jax.numpy as jnp
from jax import lax
from jax.experimental import pallas as pl
from jax.experimental.pallas import tpu as pltpu
from jax.sharding import PartitionSpec as P

TILE = 128
OTILE = 16
VMEM = pl.BlockSpec(memory_space=pltpu.VMEM)
SMEM = pl.BlockSpec(memory_space=pltpu.SMEM)
ANY = pl.BlockSpec(memory_space=pl.ANY)


def limit(*values):
    nbytes = sum(v.size * v.dtype.itemsize for v in values)
    return pltpu.CompilerParams(vmem_limit_bytes=2 * nbytes + 4 * 2**20)


def after(v, *deps):
    return lax.optimization_barrier((v, *deps))[0]


def held(v):
    return pltpu.with_memory_space_constraint(v, pltpu.VMEM)


def mask_kernel(amask, bmask, a, b, a_out, b_out):
    def factor(mask, i, j):
        return mask[i, j].astype(jnp.float32).astype(a.dtype)

    for i in range(a.shape[0] // OTILE):
        for j in range(a.shape[1] // TILE):
            at = (slice(i * OTILE, (i + 1) * OTILE), slice(j * TILE, (j + 1) * TILE))
            a_out[at] = a[at] * factor(amask, i, j)
    for i in range(b.shape[0] // TILE):
        for j in range(b.shape[1] // TILE):
            at = (slice(i * TILE, (i + 1) * TILE), slice(j * TILE, (j + 1) * TILE))
            b_out[at] = b[at] * factor(bmask, j, i)


def product(a, b, dtype):
    return (0.5 * jnp.dot(a, b, preferred_element_type=jnp.float32)).astype(dtype)


def near_kernel(masks, *refs):
    a_refs, b_refs, (a_all, near) = refs[: len(masks)], refs[len(masks) : -2], refs[-2:]
    for ks, ref in zip(masks, a_refs, strict=True):
        rows = ref.shape[0] // len(ks)
        for i, k in enumerate(ks):
            at = pl.multiple_of((lax.axis_index("grp") ^ k) * rows, OTILE)
            a_all[pl.ds(at, rows), :] = ref[i * rows : (i + 1) * rows, :]
    for n, b in enumerate(b_refs):
        near[n] = product(a_all[...], b[...], near.dtype)


def far_kernel(near_at, far_at, a_all, near, *refs):
    b_refs, (out, stage, near_sems, far_sems) = refs[:-4], refs[-4:]
    rows, width = near.shape[1:]

    def write(block, k, top, sem):
        at = pl.multiple_of((lax.axis_index("blk") ^ k) * width, TILE)
        copy = pltpu.make_async_copy(block, out.at[pl.ds(top, block.shape[0]), pl.ds(at, width)], sem)
        copy.start()
        return copy

    copies = [write(near.at[n], k, 0, near_sems.at[n]) for n, k in enumerate(near_at)]
    cuts = far_sems.shape[1]
    for n, k in enumerate(far_at):
        for c in range(cuts):
            at = pl.ds(c * (rows // cuts), rows // cuts)
            stage[n, at, :] = product(a_all[at, :], b_refs[n][...], stage.dtype)
            copies.append(write(stage.at[n, at], k, c * (rows // cuts), far_sems.at[n, c]))
    for copy in copies:
        copy.wait()


def local(n_blk, n_grp, a, b, amask, bmask):
    a_own, b_own = pl.pallas_call(
        mask_kernel,
        out_shape=[pltpu.VMEM(a.shape, a.dtype), pltpu.VMEM(b.shape, b.dtype)],
        in_specs=[SMEM, SMEM, VMEM, VMEM],
        out_specs=[VMEM, VMEM],
        compiler_params=pltpu.CompilerParams(vmem_limit_bytes=56 * 2**20),
    )(amask, bmask.T, a, b)

    def swap(v, axis, n, k):
        return lax.ppermute(v, axis, [(i, i ^ k) for i in range(n)])

    def joined(*vs):
        def join_kernel(*refs):
            top = 0
            for ref in refs[:-1]:
                refs[-1][top : top + ref.shape[0], :] = ref[...]
                top += ref.shape[0]

        rows = sum(v.shape[0] for v in vs)
        return pl.pallas_call(
            join_kernel,
            out_shape=pltpu.VMEM((rows, vs[0].shape[1]), vs[0].dtype),
            in_specs=[VMEM] * len(vs),
            out_specs=VMEM,
            compiler_params=limit(*vs),
        )(*[held(v) for v in vs])

    def line(*vs):
        done = []
        for v in vs:
            done = list(lax.optimization_barrier((v, *done)))
        return done[::-1]

    def along_grp(v, k):
        return swap(v, "grp", n_grp, k)

    def along_blk(v, k):
        return swap(v, "blk", n_blk, k)

    panels = {0: b_own} | {k: along_blk(b_own, k) for k in range(2, n_blk, 2)}
    z4, z2, z1 = along_grp(a_own, 4), along_grp(a_own, 2), along_grp(a_own, 1)
    z4, z2 = line(z4, z2)
    pair = joined(z2, z4)
    m35 = along_grp(pair, 1)
    m7 = along_grp(z4, 3)
    m6 = along_grp(after(z4, z1), 2)
    panels |= {k ^ 1: along_blk(after(v, z1), 1) for k, v in panels.items()}
    m7, m35, m6 = line(m7, m35, m6)
    shards = {(0,): a_own, (1,): z1, (2,): z2, (3, 5): m35, (4,): z4, (6,): m6, (7,): m7}
    for top in [8 << i for i in range((n_grp // 8).bit_length() - 1)]:
        shards[(top,)] = along_grp(a_own, top)
        shards |= {(top ^ k,): along_grp(shards[(top,)], k) for k in range(1, top)}
    rows, depth, width = a.shape[0] * n_grp, a.shape[1], b.shape[1]
    out = jax.ShapeDtypeStruct((rows, width * n_blk), a.dtype)
    near_at, far_at = list(range(0, n_blk, 2)), list(range(1, n_blk, 2))
    a_full, near = pl.pallas_call(
        functools.partial(near_kernel, list(shards)),
        out_shape=[pltpu.VMEM((rows, depth), a.dtype), pltpu.VMEM((len(near_at), rows, width), a.dtype)],
        in_specs=[VMEM] * (len(shards) + len(near_at)),
        out_specs=[VMEM, VMEM],
        compiler_params=limit(out),
        cost_estimate=pl.CostEstimate(flops=50 * 10**8, bytes_accessed=2**22, transcendentals=0),
    )(*[held(v) for v in [*shards.values()] + [panels[k] for k in near_at]])
    return pl.pallas_call(
        functools.partial(far_kernel, near_at, far_at),
        out_shape=out,
        in_specs=[VMEM] * (2 + len(far_at)),
        out_specs=ANY,
        scratch_shapes=[
            pltpu.VMEM((len(far_at), rows, width), a.dtype),
            pltpu.SemaphoreType.DMA((len(near_at),)),
            pltpu.SemaphoreType.DMA((len(far_at), 2)),
        ],
        compiler_params=limit(out),
    )(*[held(v) for v in [a_full, near] + [panels[k] for k in far_at]])


def solution(mesh):
    return jax.shard_map(
        functools.partial(local, mesh.shape["blk"], mesh.shape["grp"]),
        mesh=mesh,
        in_specs=(
            P(("blk", "grp"), None),
            P(None, ("grp", "blk")),
            P(("blk", "grp"), None),
            P(None, ("grp", "blk")),
        ),
        out_specs=P("blk", "grp"),
        check_vma=False,
    )
```

```python
import functools
import jax
import jax.numpy as jnp
from jax import lax
from jax.experimental import pallas as pl
from jax.experimental.pallas import tpu as pltpu
from jax.sharding import PartitionSpec as P

TILE = 128
OTILE = 16
VMEM = pl.BlockSpec(memory_space=pltpu.VMEM)
SMEM = pl.BlockSpec(memory_space=pltpu.SMEM)
ANY = pl.BlockSpec(memory_space=pl.ANY)


def limit(*values):
    nbytes = sum(v.size * v.dtype.itemsize for v in values)
    return pltpu.CompilerParams(vmem_limit_bytes=2 * nbytes + 4 * 2**20)


def after(v, *deps):
    return lax.optimization_barrier((v, *deps))[0]


def held(v):
    return pltpu.with_memory_space_constraint(v, pltpu.VMEM)


def mask_kernel(amask, bmask, a, b, a_out, b_out):
    def factor(mask, i, j):
        return mask[i, j].astype(jnp.float32).astype(a.dtype)

    for i in range(a.shape[0] // OTILE):
        for j in range(a.shape[1] // TILE):
            at = (slice(i * OTILE, (i + 1) * OTILE), slice(j * TILE, (j + 1) * TILE))
            a_out[at] = a[at] * factor(amask, i, j)
    for i in range(b.shape[0] // TILE):
        for j in range(b.shape[1] // TILE):
            at = (slice(i * TILE, (i + 1) * TILE), slice(j * TILE, (j + 1) * TILE))
            b_out[at] = b[at] * factor(bmask, j, i)


def product(a, b, dtype):
    return (0.5 * jnp.dot(a, b, preferred_element_type=jnp.float32)).astype(dtype)


def early_kernel(n_rows, *refs):
    a_refs, b_refs, (early, a_early) = refs[:n_rows], refs[n_rows:-2], refs[-2:]
    top = 0
    for ref in a_refs:
        a_early[top : top + ref.shape[0], :] = ref[...]
        top += ref.shape[0]
    for n, b in enumerate(b_refs):
        early[n] = product(a_early[...], b[...], early.dtype)


def rows_kernel(masks, late_at, *refs):
    a_refs, (_, a_all, a_late) = refs[: len(masks)], refs[len(masks) :]
    for ks, ref in zip(masks, a_refs, strict=True):
        rows = ref.shape[0] // len(ks)
        for i, k in enumerate(ks):
            at = pl.multiple_of((lax.axis_index("grp") ^ k) * rows, OTILE)
            a_all[pl.ds(at, rows), :] = ref[i * rows : (i + 1) * rows, :]
            if k in late_at:
                top = late_at.index(k) * rows
                a_late[top : top + rows, :] = ref[i * rows : (i + 1) * rows, :]


def write_kernel(early_at, late_at, near_at, far_at, a_all, a_late, early, *refs):
    b_refs, (out, stage, sems) = dict(zip(near_at + far_at, refs[:-3], strict=True)), refs[-3:]
    tall, width = stage.shape[1:]
    rows = tall // (len(early_at) + len(late_at))
    copies = []

    def write(k, top, height, sem):
        col = pl.multiple_of((lax.axis_index("blk") ^ k) * width, TILE)
        part = stage.at[k, top : top + height]
        copies.append(pltpu.make_async_copy(part, out.at[top : top + height, pl.ds(col, width)], sem))
        copies[-1].start()

    for n, k in enumerate(near_at):
        late = product(a_late[...], b_refs[k][...], stage.dtype)
        for at, found in ((early_at, early[n]), (late_at, late)):
            for i, m in enumerate(at):
                row = pl.multiple_of((lax.axis_index("grp") ^ m) * rows, OTILE)
                stage[k, pl.ds(row, rows), :] = found[i * rows : (i + 1) * rows]
        write(k, 0, tall, sems.at[k, 0])
    for k in far_at:
        for c in range(2):
            top, height = c * (tall // 2), tall // 2
            stage[k, top : top + height] = product(a_all[top : top + height], b_refs[k][...], stage.dtype)
            write(k, top, height, sems.at[k, c])
    for copy in copies:
        copy.wait()


def local(n_blk, n_grp, a, b, amask, bmask):
    a_own, b_own = pl.pallas_call(
        mask_kernel,
        out_shape=[pltpu.VMEM(a.shape, a.dtype), pltpu.VMEM(b.shape, b.dtype)],
        in_specs=[SMEM, SMEM, VMEM, VMEM],
        out_specs=[VMEM, VMEM],
        compiler_params=pltpu.CompilerParams(vmem_limit_bytes=56 * 2**20),
    )(amask, bmask.T, a, b)

    def swap(v, axis, n, k):
        return lax.ppermute(v, axis, [(i, i ^ k) for i in range(n)])

    def joined(*vs):
        def join_kernel(*refs):
            top = 0
            for ref in refs[:-1]:
                refs[-1][top : top + ref.shape[0], :] = ref[...]
                top += ref.shape[0]

        rows = sum(v.shape[0] for v in vs)
        return pl.pallas_call(
            join_kernel,
            out_shape=pltpu.VMEM((rows, vs[0].shape[1]), vs[0].dtype),
            in_specs=[VMEM] * len(vs),
            out_specs=VMEM,
            compiler_params=limit(*vs),
        )(*[held(v) for v in vs])

    def line(*vs):
        done = []
        for v in vs:
            done = list(lax.optimization_barrier((v, *done)))
        return done[::-1]

    def along_grp(v, k):
        return swap(v, "grp", n_grp, k)

    def along_blk(v, k):
        return swap(v, "blk", n_blk, k)

    panels = {0: b_own} | {k: along_blk(b_own, k) for k in range(2, n_blk, 2)}
    z4, z2, z1 = along_grp(a_own, 4), along_grp(a_own, 2), along_grp(a_own, 1)
    z4, z2 = line(z4, z2)
    pair = joined(z2, z4)
    m35 = along_grp(pair, 1)
    m7 = along_grp(z4, 3)
    m6 = along_grp(after(z4, z1), 2)
    first = {0: a_own, 1: z1, 2: z2, 4: z4}
    rows, depth, width = a.shape[0] * n_grp, a.shape[1], b.shape[1]
    out = jax.ShapeDtypeStruct((rows, width * n_blk), a.dtype)
    near_at = tuple(range(0, n_blk, 2))
    far_at = tuple(k for k in range(n_blk) if k not in near_at)
    early_at = (0, 1, 2, 4)
    late_at = tuple(k for k in range(n_grp) if k not in early_at)
    tall = a.shape[0] * len(early_at)
    soon = [first[k] for k in early_at] + [panels[k] for k in near_at]
    early = pl.pallas_call(
        functools.partial(early_kernel, len(early_at)),
        out_shape=pltpu.VMEM((len(near_at), tall, width), a.dtype),
        in_specs=[VMEM] * len(soon),
        out_specs=VMEM,
        scratch_shapes=[pltpu.VMEM((tall, depth), a.dtype)],
        compiler_params=limit(out),
        cost_estimate=pl.CostEstimate(flops=10**6, bytes_accessed=2**20, transcendentals=0),
    )(*[held(v) for v in soon])
    panels |= {k ^ 1: along_blk(after(v, z1, early) if k else after(v, z1), 1) for k, v in panels.items()}
    m7, m35, m6 = line(m7, m35, m6)
    shards = {(0,): a_own, (1,): z1, (2,): z2, (3, 5): m35, (4,): z4, (6,): m6, (7,): m7}
    for top in [8 << i for i in range((n_grp // 8).bit_length() - 1)]:
        shards[(top,)] = along_grp(a_own, top)
        shards |= {(top ^ k,): along_grp(shards[(top,)], k) for k in range(1, top)}
    a_all, a_late = pl.pallas_call(
        functools.partial(rows_kernel, list(shards), late_at),
        out_shape=[pltpu.VMEM((rows, depth), a.dtype), pltpu.VMEM((rows - tall, depth), a.dtype)],
        in_specs=[VMEM] * (len(shards) + 1),
        out_specs=[VMEM, VMEM],
        compiler_params=limit(out),
        cost_estimate=pl.CostEstimate(flops=52 * 10**8, bytes_accessed=2**22, transcendentals=0),
    )(*[held(v) for v in [*shards.values(), early]])
    ops = [a_all, a_late, early] + [panels[k] for k in near_at + far_at]
    return pl.pallas_call(
        functools.partial(write_kernel, early_at, late_at, near_at, far_at),
        out_shape=out,
        in_specs=[VMEM] * len(ops),
        out_specs=ANY,
        scratch_shapes=[pltpu.VMEM((n_blk, rows, width), a.dtype), pltpu.SemaphoreType.DMA((n_blk, 2))],
        compiler_params=limit(out),
    )(*[held(v) for v in ops])


def solution(mesh):
    return jax.shard_map(
        functools.partial(local, mesh.shape["blk"], mesh.shape["grp"]),
        mesh=mesh,
        in_specs=(
            P(("blk", "grp"), None),
            P(None, ("grp", "blk")),
            P(("blk", "grp"), None),
            P(None, ("grp", "blk")),
        ),
        out_specs=P("blk", "grp"),
        check_vma=False,
    )
```

```python
import functools
import jax
import jax.numpy as jnp
from jax import lax
from jax.experimental import pallas as pl
from jax.experimental.pallas import tpu as pltpu
from jax.sharding import PartitionSpec as P

TILE = 128
OTILE = 16
VMEM = pl.BlockSpec(memory_space=pltpu.VMEM)
SMEM = pl.BlockSpec(memory_space=pltpu.SMEM)
ANY = pl.BlockSpec(memory_space=pl.ANY)


def limit(*values):
    nbytes = sum(v.size * v.dtype.itemsize for v in values)
    return pltpu.CompilerParams(vmem_limit_bytes=2 * nbytes + 4 * 2**20)


def after(v, *deps):
    return lax.optimization_barrier((v, *deps))[0]


def held(v):
    return pltpu.with_memory_space_constraint(v, pltpu.VMEM)


def mask_kernel(amask, bmask, a, b, a_out, b_out, amask_here, bmask_here, a_here, b_here, sems):
    depth = b.shape[0] // 2
    pieces = [pl.ds(i * depth, depth) for i in range(2)]
    moves = [(amask, amask_here), (bmask, bmask_here), (a, a_here)]
    moves += [(b.at[piece], b_here.at[piece]) for piece in pieces]
    copies = [pltpu.make_async_copy(*move, sems.at[i]) for i, move in enumerate(moves)]
    for copy in copies:
        copy.start()

    def masked(v, mask, i, j):
        return v * mask[i, j].astype(jnp.float32).astype(v.dtype)

    for copy in copies[:3]:
        copy.wait()
    for i in range(a.shape[0] // OTILE):
        for j in range(a.shape[1] // TILE):
            at = (slice(i * OTILE, (i + 1) * OTILE), slice(j * TILE, (j + 1) * TILE))
            a_out[at] = masked(a_here[at], amask_here, i, j)
    for i in range(b.shape[0] // TILE):
        if i * TILE % depth == 0:
            copies[3 + i * TILE // depth].wait()
        for j in range(b.shape[1] // TILE):
            at = (slice(i * TILE, (i + 1) * TILE), slice(j * TILE, (j + 1) * TILE))
            b_out[at] = masked(b_here[at], bmask_here, j, i)


def product(a, b, dtype):
    return (0.5 * jnp.dot(a, b, preferred_element_type=jnp.float32)).astype(dtype)


def early_kernel(n_rows, *refs):
    a_refs, b_refs, (early, a_early) = refs[:n_rows], refs[n_rows:-2], refs[-2:]
    top = 0
    for ref in a_refs:
        a_early[top : top + ref.shape[0], :] = ref[...]
        top += ref.shape[0]
    for n, b in enumerate(b_refs):
        early[n] = product(a_early[...], b[...], early.dtype)


def rows_kernel(masks, late_at, *refs):
    a_refs, (_, a_all, a_late) = refs[: len(masks)], refs[len(masks) :]
    for ks, ref in zip(masks, a_refs, strict=True):
        rows = ref.shape[0] // len(ks)
        for i, k in enumerate(ks):
            at = pl.multiple_of((lax.axis_index("grp") ^ k) * rows, OTILE)
            a_all[pl.ds(at, rows), :] = ref[i * rows : (i + 1) * rows, :]
            if k in late_at:
                top = late_at.index(k) * rows
                a_late[top : top + rows, :] = ref[i * rows : (i + 1) * rows, :]


def write_kernel(early_at, late_at, near_at, far_at, a_all, a_late, early, *refs):
    b_refs, (out, stage, sems) = dict(zip(near_at + far_at, refs[:-3], strict=True)), refs[-3:]
    tall, width = stage.shape[1:]
    rows = tall // (len(early_at) + len(late_at))
    copies = []

    def write(k, top, height, sem):
        col = pl.multiple_of((lax.axis_index("blk") ^ k) * width, TILE)
        part = stage.at[k, top : top + height]
        copies.append(pltpu.make_async_copy(part, out.at[top : top + height, pl.ds(col, width)], sem))
        copies[-1].start()

    for n, k in enumerate(near_at):
        late = product(a_late[...], b_refs[k][...], stage.dtype)
        for at, found in ((early_at, early[n]), (late_at, late)):
            for i, m in enumerate(at):
                row = pl.multiple_of((lax.axis_index("grp") ^ m) * rows, OTILE)
                stage[k, pl.ds(row, rows), :] = found[i * rows : (i + 1) * rows]
        write(k, 0, tall, sems.at[k, 0])
    for k in far_at:
        for c in range(2):
            top, height = c * (tall // 2), tall // 2
            stage[k, top : top + height] = product(a_all[top : top + height], b_refs[k][...], stage.dtype)
            write(k, top, height, sems.at[k, c])
    for copy in copies:
        copy.wait()


def local(n_blk, n_grp, a, b, amask, bmask):
    a_own, b_own = pl.pallas_call(
        mask_kernel,
        out_shape=[pltpu.VMEM(a.shape, a.dtype), pltpu.VMEM(b.shape, b.dtype)],
        in_specs=[ANY] * 4,
        out_specs=[VMEM, VMEM],
        scratch_shapes=[
            pltpu.SMEM(amask.shape, amask.dtype),
            pltpu.SMEM(bmask.shape[::-1], bmask.dtype),
            pltpu.VMEM(a.shape, a.dtype),
            pltpu.VMEM(b.shape, b.dtype),
            pltpu.SemaphoreType.DMA((2 + 3,)),
        ],
        compiler_params=pltpu.CompilerParams(vmem_limit_bytes=56 * 2**20),
    )(amask, bmask.T, a, b)

    def swap(v, axis, n, k):
        return lax.ppermute(v, axis, [(i, i ^ k) for i in range(n)])

    def joined(*vs):
        def join_kernel(*refs):
            top = 0
            for ref in refs[:-1]:
                refs[-1][top : top + ref.shape[0], :] = ref[...]
                top += ref.shape[0]

        rows = sum(v.shape[0] for v in vs)
        return pl.pallas_call(
            join_kernel,
            out_shape=pltpu.VMEM((rows, vs[0].shape[1]), vs[0].dtype),
            in_specs=[VMEM] * len(vs),
            out_specs=VMEM,
            compiler_params=limit(*vs),
        )(*[held(v) for v in vs])

    def line(*vs):
        done = []
        for v in vs:
            done = list(lax.optimization_barrier((v, *done)))
        return done[::-1]

    def along_grp(v, k):
        return swap(v, "grp", n_grp, k)

    def along_blk(v, k):
        return swap(v, "blk", n_blk, k)

    panels = {0: b_own} | {k: along_blk(b_own, k) for k in range(2, n_blk, 2)}
    z4, z2, z1 = along_grp(a_own, 4), along_grp(a_own, 2), along_grp(a_own, 1)
    z4, z2 = line(z4, z2)
    pair = joined(z2, z4)
    m35 = along_grp(pair, 1)
    m7 = along_grp(z4, 3)
    m6 = along_grp(after(z4, z1), 2)
    first = {0: a_own, 1: z1, 2: z2, 4: z4}
    rows, depth, width = a.shape[0] * n_grp, a.shape[1], b.shape[1]
    out = jax.ShapeDtypeStruct((rows, width * n_blk), a.dtype)
    near_at = tuple(range(0, n_blk, 2))
    far_at = tuple(k for k in range(n_blk) if k not in near_at)
    early_at = (0, 1, 2, 4)
    late_at = tuple(k for k in range(n_grp) if k not in early_at)
    tall = a.shape[0] * len(early_at)
    soon = [first[k] for k in early_at] + [panels[k] for k in near_at]
    early = pl.pallas_call(
        functools.partial(early_kernel, len(early_at)),
        out_shape=pltpu.VMEM((len(near_at), tall, width), a.dtype),
        in_specs=[VMEM] * len(soon),
        out_specs=VMEM,
        scratch_shapes=[pltpu.VMEM((tall, depth), a.dtype)],
        compiler_params=limit(out),
        cost_estimate=pl.CostEstimate(flops=10**6, bytes_accessed=2**20, transcendentals=0),
    )(*[held(v) for v in soon])
    panels |= {k ^ 1: along_blk(after(v, z1, early) if k else after(v, z1), 1) for k, v in panels.items()}
    m7, m35, m6 = line(m7, m35, m6)
    shards = {(0,): a_own, (1,): z1, (2,): z2, (3, 5): m35, (4,): z4, (6,): m6, (7,): m7}
    for top in [8 << i for i in range((n_grp // 8).bit_length() - 1)]:
        shards[(top,)] = along_grp(a_own, top)
        shards |= {(top ^ k,): along_grp(shards[(top,)], k) for k in range(1, top)}
    a_all, a_late = pl.pallas_call(
        functools.partial(rows_kernel, list(shards), late_at),
        out_shape=[pltpu.VMEM((rows, depth), a.dtype), pltpu.VMEM((rows - tall, depth), a.dtype)],
        in_specs=[VMEM] * (len(shards) + 1),
        out_specs=[VMEM, VMEM],
        compiler_params=limit(out),
        cost_estimate=pl.CostEstimate(flops=52 * 10**8, bytes_accessed=2**22, transcendentals=0),
    )(*[held(v) for v in [*shards.values(), early]])
    ops = [a_all, a_late, early] + [panels[k] for k in near_at + far_at]
    return pl.pallas_call(
        functools.partial(write_kernel, early_at, late_at, near_at, far_at),
        out_shape=out,
        in_specs=[VMEM] * len(ops),
        out_specs=ANY,
        scratch_shapes=[pltpu.VMEM((n_blk, rows, width), a.dtype), pltpu.SemaphoreType.DMA((n_blk, 2))],
        compiler_params=limit(out),
    )(*[held(v) for v in ops])


def solution(mesh):
    return jax.shard_map(
        functools.partial(local, mesh.shape["blk"], mesh.shape["grp"]),
        mesh=mesh,
        in_specs=(
            P(("blk", "grp"), None),
            P(None, ("grp", "blk")),
            P(("blk", "grp"), None),
            P(None, ("grp", "blk")),
        ),
        out_specs=P("blk", "grp"),
        check_vma=False,
    )
```

```python
import functools
import jax
import jax.numpy as jnp
from jax import lax
from jax.experimental import pallas as pl
from jax.experimental.pallas import tpu as pltpu
from jax.sharding import PartitionSpec as P

TILE = 128
OTILE = 16
VMEM = pl.BlockSpec(memory_space=pltpu.VMEM)
SMEM = pl.BlockSpec(memory_space=pltpu.SMEM)
ANY = pl.BlockSpec(memory_space=pl.ANY)


def limit(*values):
    nbytes = sum(v.size * v.dtype.itemsize for v in values)
    return pltpu.CompilerParams(vmem_limit_bytes=2 * nbytes + 4 * 2**20)


def after(v, *deps):
    return lax.optimization_barrier((v, *deps))[0]


def held(v):
    return pltpu.with_memory_space_constraint(v, pltpu.VMEM)


def mask_kernel(amask, bmask, a, b, a_out, b_out, amask_here, bmask_here, a_here, b_here, sems):
    depth = b.shape[0] // 2
    pieces = [pl.ds(i * depth, depth) for i in range(2)]
    moves = [(amask, amask_here), (bmask, bmask_here), (a, a_here)]
    moves += [(b.at[piece], b_here.at[piece]) for piece in pieces]
    copies = [pltpu.make_async_copy(*move, sems.at[i]) for i, move in enumerate(moves)]
    for copy in copies:
        copy.start()

    def masked(v, mask, i, j):
        return v * mask[i, j].astype(jnp.float32).astype(v.dtype)

    for copy in copies[:3]:
        copy.wait()
    for i in range(a.shape[0] // OTILE):
        for j in range(a.shape[1] // TILE):
            at = (slice(i * OTILE, (i + 1) * OTILE), slice(j * TILE, (j + 1) * TILE))
            a_out[at] = masked(a_here[at], amask_here, i, j)
    for i in range(b.shape[0] // TILE):
        if i * TILE % depth == 0:
            copies[3 + i * TILE // depth].wait()
        for j in range(b.shape[1] // TILE):
            at = (slice(i * TILE, (i + 1) * TILE), slice(j * TILE, (j + 1) * TILE))
            b_out[at] = masked(b_here[at], bmask_here, j, i)


def product(a, b, dtype):
    return (0.5 * jnp.dot(a, b, preferred_element_type=jnp.float32)).astype(dtype)


def early_kernel(n_rows, *refs):
    a_refs, b_refs, (early, a_early) = refs[:n_rows], refs[n_rows:-2], refs[-2:]
    top = 0
    for ref in a_refs:
        a_early[top : top + ref.shape[0], :] = ref[...]
        top += ref.shape[0]
    for n, b in enumerate(b_refs):
        early[n] = product(a_early[...], b[...], early.dtype)


def rows_kernel(masks, late_at, *refs):
    a_refs, (_, a_all, a_late) = refs[: len(masks)], refs[len(masks) :]
    for ks, ref in zip(masks, a_refs, strict=True):
        rows = ref.shape[0] // len(ks)
        for i, k in enumerate(ks):
            at = pl.multiple_of((lax.axis_index("grp") ^ k) * rows, OTILE)
            a_all[pl.ds(at, rows), :] = ref[i * rows : (i + 1) * rows, :]
            if k in late_at:
                top = late_at.index(k) * rows
                a_late[top : top + rows, :] = ref[i * rows : (i + 1) * rows, :]


def write_kernel(early_at, late_at, near_at, far_at, a_all, a_late, early_own, early, *refs):
    b_refs, (out, stage, sems) = dict(zip(near_at + far_at, refs[:-3], strict=True)), refs[-3:]
    tall, width = stage.shape[1:]
    rows = tall // (len(early_at) + len(late_at))
    copies = []

    def write(k, top, height, sem):
        col = pl.multiple_of((lax.axis_index("blk") ^ k) * width, TILE)
        part = stage.at[k, top : top + height]
        copies.append(pltpu.make_async_copy(part, out.at[top : top + height, pl.ds(col, width)], sem))
        copies[-1].start()

    for n, k in enumerate(near_at):
        begun = early[n - 1] if n else early_own[0]
        late = product(a_late[...], b_refs[k][...], stage.dtype)
        for at, found in ((early_at, begun), (late_at, late)):
            for i, m in enumerate(at):
                row = pl.multiple_of((lax.axis_index("grp") ^ m) * rows, OTILE)
                stage[k, pl.ds(row, rows), :] = found[i * rows : (i + 1) * rows]
        write(k, 0, tall, sems.at[k, 0])
    for k in far_at:
        for c in range(2):
            top, height = c * (tall // 2), tall // 2
            stage[k, top : top + height] = product(a_all[top : top + height], b_refs[k][...], stage.dtype)
            write(k, top, height, sems.at[k, c])
    for copy in copies:
        copy.wait()


def local(n_blk, n_grp, a, b, amask, bmask):
    a_own, b_own = pl.pallas_call(
        mask_kernel,
        out_shape=[pltpu.VMEM(a.shape, a.dtype), pltpu.VMEM(b.shape, b.dtype)],
        in_specs=[ANY] * 4,
        out_specs=[VMEM, VMEM],
        scratch_shapes=[
            pltpu.SMEM(amask.shape, amask.dtype),
            pltpu.SMEM(bmask.shape[::-1], bmask.dtype),
            pltpu.VMEM(a.shape, a.dtype),
            pltpu.VMEM(b.shape, b.dtype),
            pltpu.SemaphoreType.DMA((2 + 3,)),
        ],
        compiler_params=pltpu.CompilerParams(vmem_limit_bytes=56 * 2**20),
    )(amask, bmask.T, a, b)

    def swap(v, axis, n, k):
        return lax.ppermute(v, axis, [(i, i ^ k) for i in range(n)])

    def joined(*vs):
        def join_kernel(*refs):
            top = 0
            for ref in refs[:-1]:
                refs[-1][top : top + ref.shape[0], :] = ref[...]
                top += ref.shape[0]

        rows = sum(v.shape[0] for v in vs)
        return pl.pallas_call(
            join_kernel,
            out_shape=pltpu.VMEM((rows, vs[0].shape[1]), vs[0].dtype),
            in_specs=[VMEM] * len(vs),
            out_specs=VMEM,
            compiler_params=limit(*vs),
        )(*[held(v) for v in vs])

    def line(*vs):
        done = []
        for v in vs:
            done = list(lax.optimization_barrier((v, *done)))
        return done[::-1]

    def along_grp(v, k):
        return swap(v, "grp", n_grp, k)

    def along_blk(v, k):
        return swap(v, "blk", n_blk, k)

    panels = {0: b_own} | {k: along_blk(b_own, k) for k in range(2, n_blk, 2)}
    z4, z2, z1 = along_grp(a_own, 4), along_grp(a_own, 2), along_grp(a_own, 1)
    z4, z2 = line(z4, z2)
    pair = joined(z2, z4)
    m35 = along_grp(pair, 1)
    m7 = along_grp(z4, 3)
    m6 = along_grp(after(z4, z1), 2)
    first = {0: a_own, 1: z1, 2: z2, 4: z4}
    rows, depth, width = a.shape[0] * n_grp, a.shape[1], b.shape[1]
    out = jax.ShapeDtypeStruct((rows, width * n_blk), a.dtype)
    near_at = tuple(range(0, n_blk, 2))
    far_at = tuple(k for k in range(n_blk) if k not in near_at)
    early_at = (0, 1, 2, 4)
    late_at = tuple(k for k in range(n_grp) if k not in early_at)
    tall = a.shape[0] * len(early_at)
    soon = [first[k] for k in early_at]

    def begun(at):
        ops = soon + [panels[k] for k in at]
        return pl.pallas_call(
            functools.partial(early_kernel, len(soon)),
            out_shape=pltpu.VMEM((len(at), tall, width), a.dtype),
            in_specs=[VMEM] * len(ops),
            out_specs=VMEM,
            scratch_shapes=[pltpu.VMEM((tall, depth), a.dtype)],
            compiler_params=limit(out),
            cost_estimate=pl.CostEstimate(flops=10**6, bytes_accessed=2**20, transcendentals=0),
        )(*[held(v) for v in ops])

    early_own, early = begun(near_at[:1]), begun(near_at[1:])
    panels |= {k ^ 1: along_blk(after(v, z1, early) if k else after(v, z1), 1) for k, v in panels.items()}
    m7, m35, m6 = line(m7, m35, m6)
    shards = {(0,): a_own, (1,): z1, (2,): z2, (3, 5): m35, (4,): z4, (6,): m6, (7,): m7}
    for top in [8 << i for i in range((n_grp // 8).bit_length() - 1)]:
        shards[(top,)] = along_grp(a_own, top)
        shards |= {(top ^ k,): along_grp(shards[(top,)], k) for k in range(1, top)}
    a_all, a_late = pl.pallas_call(
        functools.partial(rows_kernel, list(shards), late_at),
        out_shape=[pltpu.VMEM((rows, depth), a.dtype), pltpu.VMEM((rows - tall, depth), a.dtype)],
        in_specs=[VMEM] * (len(shards) + 1),
        out_specs=[VMEM, VMEM],
        compiler_params=limit(out),
        cost_estimate=pl.CostEstimate(flops=52 * 10**8, bytes_accessed=2**22, transcendentals=0),
    )(*[held(v) for v in [*shards.values(), early]])
    ops = [a_all, a_late, early_own, early] + [panels[k] for k in near_at + far_at]
    return pl.pallas_call(
        functools.partial(write_kernel, early_at, late_at, near_at, far_at),
        out_shape=out,
        in_specs=[VMEM] * len(ops),
        out_specs=ANY,
        scratch_shapes=[pltpu.VMEM((n_blk, rows, width), a.dtype), pltpu.SemaphoreType.DMA((n_blk, 2))],
        compiler_params=limit(out),
    )(*[held(v) for v in ops])


def solution(mesh):
    return jax.shard_map(
        functools.partial(local, mesh.shape["blk"], mesh.shape["grp"]),
        mesh=mesh,
        in_specs=(
            P(("blk", "grp"), None),
            P(None, ("grp", "blk")),
            P(("blk", "grp"), None),
            P(None, ("grp", "blk")),
        ),
        out_specs=P("blk", "grp"),
        check_vma=False,
    )
```

```python
import functools
import jax
import jax.numpy as jnp
from jax import lax
from jax.experimental import pallas as pl
from jax.experimental.pallas import tpu as pltpu
from jax.sharding import PartitionSpec as P

TILE = 128
OTILE = 16
VMEM = pl.BlockSpec(memory_space=pltpu.VMEM)
SMEM = pl.BlockSpec(memory_space=pltpu.SMEM)
ANY = pl.BlockSpec(memory_space=pl.ANY)


def limit(*values):
    nbytes = sum(v.size * v.dtype.itemsize for v in values)
    return pltpu.CompilerParams(vmem_limit_bytes=2 * nbytes + 4 * 2**20)


def after(v, *deps):
    return lax.optimization_barrier((v, *deps))[0]


def held(v):
    return pltpu.with_memory_space_constraint(v, pltpu.VMEM)


def mask_kernel(amask, bmask, a, b, a_out, b_out, amask_here, bmask_here, a_here, b_here, sems):
    depth = b.shape[0] // 2
    pieces = [pl.ds(i * depth, depth) for i in range(2)]
    moves = [(amask, amask_here), (bmask, bmask_here), (a, a_here)]
    moves += [(b.at[piece], b_here.at[piece]) for piece in pieces]
    copies = [pltpu.make_async_copy(*move, sems.at[i]) for i, move in enumerate(moves)]
    for copy in copies:
        copy.start()

    def masked(v, mask, i, j):
        return v * mask[i, j].astype(jnp.float32).astype(v.dtype)

    for copy in copies[:3]:
        copy.wait()
    for i in range(a.shape[0] // OTILE):
        for j in range(a.shape[1] // TILE):
            at = (slice(i * OTILE, (i + 1) * OTILE), slice(j * TILE, (j + 1) * TILE))
            a_out[at] = masked(a_here[at], amask_here, i, j)
    for i in range(b.shape[0] // TILE):
        if i * TILE % depth == 0:
            copies[3 + i * TILE // depth].wait()
        for j in range(b.shape[1] // TILE):
            at = (slice(i * TILE, (i + 1) * TILE), slice(j * TILE, (j + 1) * TILE))
            b_out[at] = masked(b_here[at], bmask_here, j, i)


def product(a, b, dtype):
    return (0.5 * jnp.dot(a, b, preferred_element_type=jnp.float32)).astype(dtype)


def early_kernel(n_rows, *refs):
    a_refs, b_refs, (early, a_early) = refs[:n_rows], refs[n_rows:-2], refs[-2:]
    top = 0
    for ref in a_refs:
        a_early[top : top + ref.shape[0], :] = ref[...]
        top += ref.shape[0]
    for n, b in enumerate(b_refs):
        early[n] = product(a_early[...], b[...], early.dtype)


def rows_kernel(masks, late_at, *refs):
    a_refs, (_, a_all, a_late) = refs[: len(masks)], refs[len(masks) :]
    for ks, ref in zip(masks, a_refs, strict=True):
        rows = ref.shape[0] // len(ks)
        for i, k in enumerate(ks):
            at = pl.multiple_of((lax.axis_index("grp") ^ k) * rows, OTILE)
            a_all[pl.ds(at, rows), :] = ref[i * rows : (i + 1) * rows, :]
            if k in late_at:
                top = late_at.index(k) * rows
                a_late[top : top + rows, :] = ref[i * rows : (i + 1) * rows, :]


def write_kernel(early_at, late_at, near_at, far_at, a_all, a_late, early, *refs):
    b_refs, (out, stage, sems) = dict(zip(near_at + far_at, refs[:-3], strict=True)), refs[-3:]
    tall, width = stage.shape[1:]
    rows = tall // (len(early_at) + len(late_at))
    copies = []

    def write(k, top, height, sem):
        col = pl.multiple_of((lax.axis_index("blk") ^ k) * width, TILE)
        part = stage.at[k, top : top + height]
        copies.append(pltpu.make_async_copy(part, out.at[top : top + height, pl.ds(col, width)], sem))
        copies[-1].start()

    for n, k in enumerate(near_at):
        late = product(a_late[...], b_refs[k][...], stage.dtype)
        for at, found in ((early_at, early[n]), (late_at, late)):
            for i, m in enumerate(at):
                row = pl.multiple_of((lax.axis_index("grp") ^ m) * rows, OTILE)
                stage[k, pl.ds(row, rows), :] = found[i * rows : (i + 1) * rows]
        write(k, 0, tall, sems.at[k, 0])
    for k in far_at:
        for c in range(2):
            top, height = c * (tall // 2), tall // 2
            stage[k, top : top + height] = product(a_all[top : top + height], b_refs[k][...], stage.dtype)
            write(k, top, height, sems.at[k, c])
    for copy in copies:
        copy.wait()


def local(n_blk, n_grp, a, b, amask, bmask):
    a_own, b_own = pl.pallas_call(
        mask_kernel,
        out_shape=[pltpu.VMEM(a.shape, a.dtype), pltpu.VMEM(b.shape, b.dtype)],
        in_specs=[ANY] * 4,
        out_specs=[VMEM, VMEM],
        scratch_shapes=[
            pltpu.SMEM(amask.shape, amask.dtype),
            pltpu.SMEM(bmask.shape[::-1], bmask.dtype),
            pltpu.VMEM(a.shape, a.dtype),
            pltpu.VMEM(b.shape, b.dtype),
            pltpu.SemaphoreType.DMA((2 + 3,)),
        ],
        compiler_params=pltpu.CompilerParams(vmem_limit_bytes=56 * 2**20),
    )(amask, bmask.T, a, b)

    def swap(v, axis, n, k):
        return lax.ppermute(v, axis, [(i, i ^ k) for i in range(n)])

    def joined(*vs, flops=10**6):
        def join_kernel(*refs):
            top = 0
            for ref in refs[:-1]:
                refs[-1][top : top + ref.shape[0], :] = ref[...]
                top += ref.shape[0]

        rows = sum(v.shape[0] for v in vs)
        return pl.pallas_call(
            join_kernel,
            out_shape=pltpu.VMEM((rows, vs[0].shape[1]), vs[0].dtype),
            in_specs=[VMEM] * len(vs),
            out_specs=VMEM,
            compiler_params=limit(*vs),
            cost_estimate=pl.CostEstimate(flops=flops, bytes_accessed=2**18, transcendentals=0),
        )(*[held(v) for v in vs])

    def line(*vs):
        done = []
        for v in vs:
            done = list(lax.optimization_barrier((v, *done)))
        return done[::-1]

    def along_grp(v, k):
        return swap(v, "grp", n_grp, k)

    def along_blk(v, k):
        return swap(v, "blk", n_blk, k)

    panels = {0: b_own} | {k: along_blk(b_own, k) for k in range(2, n_blk, 2)}
    z4, z1 = along_grp(a_own, 4), along_grp(a_own, 1)
    a2 = along_grp(joined(a_own, z1), 2)
    z4_on = joined(z4, flops=12 * 10**8)
    m7, m5, m6 = along_grp(z4_on, 3), along_grp(z4_on, 1), along_grp(z4_on, 2)
    rows, depth, width = a.shape[0] * n_grp, a.shape[1], b.shape[1]
    out = jax.ShapeDtypeStruct((rows, width * n_blk), a.dtype)
    near_at = tuple(range(0, n_blk, 2))
    far_at = tuple(k for k in range(n_blk) if k not in near_at)
    early_at = (0, 1, 2, 3, 4)
    late_at = tuple(k for k in range(n_grp) if k not in early_at)
    tall = a.shape[0] * len(early_at)
    soon = [a_own, z1, a2, z4] + [panels[k] for k in near_at]
    early = pl.pallas_call(
        functools.partial(early_kernel, 4),
        out_shape=pltpu.VMEM((len(near_at), tall, width), a.dtype),
        in_specs=[VMEM] * len(soon),
        out_specs=VMEM,
        scratch_shapes=[pltpu.VMEM((tall, depth), a.dtype)],
        compiler_params=limit(out),
        cost_estimate=pl.CostEstimate(flops=10**6, bytes_accessed=2**20, transcendentals=0),
    )(*[held(v) for v in soon])
    panels |= {k ^ 1: along_blk(after(v, early) if k else after(v, a2), 1) for k, v in panels.items()}
    a2, m7, m5, m6 = line(a2, m7, m5, m6)
    shards = {(0,): a_own, (1,): z1, (2, 3): a2, (4,): z4, (5,): m5, (6,): m6, (7,): m7}
    for top in [8 << i for i in range((n_grp // 8).bit_length() - 1)]:
        shards[(top,)] = along_grp(a_own, top)
        shards |= {(top ^ k,): along_grp(shards[(top,)], k) for k in range(1, top)}
    a_all, a_late = pl.pallas_call(
        functools.partial(rows_kernel, list(shards), late_at),
        out_shape=[pltpu.VMEM((rows, depth), a.dtype), pltpu.VMEM((rows - tall, depth), a.dtype)],
        in_specs=[VMEM] * (len(shards) + 1),
        out_specs=[VMEM, VMEM],
        compiler_params=limit(out),
        cost_estimate=pl.CostEstimate(flops=52 * 10**8, bytes_accessed=2**22, transcendentals=0),
    )(*[held(v) for v in [*shards.values(), early]])
    ops = [a_all, a_late, early] + [panels[k] for k in near_at + far_at]
    return pl.pallas_call(
        functools.partial(write_kernel, early_at, late_at, near_at, far_at),
        out_shape=out,
        in_specs=[VMEM] * len(ops),
        out_specs=ANY,
        scratch_shapes=[pltpu.VMEM((n_blk, rows, width), a.dtype), pltpu.SemaphoreType.DMA((n_blk, 2))],
        compiler_params=limit(out),
    )(*[held(v) for v in ops])


def solution(mesh):
    return jax.shard_map(
        functools.partial(local, mesh.shape["blk"], mesh.shape["grp"]),
        mesh=mesh,
        in_specs=(
            P(("blk", "grp"), None),
            P(None, ("grp", "blk")),
            P(("blk", "grp"), None),
            P(None, ("grp", "blk")),
        ),
        out_specs=P("blk", "grp"),
        check_vma=False,
    )
```
